32 devices in a mesh: rows: 16 (over z, y, x), cls: 2 (over core).
Axes of the slice: x: 2, y: 2, z: 4, core: 2. Of those that a mesh axis runs over, the one named last changes fastest.
Arguments:
- logits: float32 [65536, 1024], P('rows', 'cls'), may hold values from -24 to 360, as said below
- leaf_index: int32 [65536], P('rows'), may hold values from 0 to 127
- labels: int32 [65536], P('rows'), may hold values from 0 to 1023
Outputs:
- leaf_values: float32 [128, 1024], P(None, 'cls')
- updated: float32 [65536, 1024], P('rows', 'cls')
The draws below stay inside these ranges and needn't reach their ends.
Inputs may be any that keep to these rules, and one draw needn't show every extreme that they name: `logits`: raw scores of a model in training.
All inputs are finite; a program needn't handle non-finite values.
Results may differ from the reference program's by a relative error of at most 0.0003.
Values sent between devices are 32-bit elements; how exact they have to be, the bound alone decides.
No kernel may reach another device: no remote copies, remote signals or barrier semaphores. Data moves between devices by JAX's collectives and lax.ppermute only.
A program may use at most 64 MiB of HBM per device.

```python
import jax
import jax.numpy as jnp
from jax import lax

C = 1024
LEAVES = 128
ROW_DEV = 4096
ROWS = 65536
N_ROWS = 16


def draw_logits(key, part):
    first = jax.random.fold_in(key, 0)
    return jnp.clip(3.0 * jax.random.normal(first, (ROWS, C), jnp.float32), -24.0, 24.0)


def touch_ends(array, own_key, least, largest):
    extent = array.shape
    index_at = [jax.random.randint(jax.random.fold_in(own_key, axis), (), 0, extent[axis]) for axis in range(len(extent))]
    array = array.at[tuple(index_at)].set(least)
    longest = extent.index(max(extent))
    index_at[longest] = (index_at[longest] + 1) % extent[longest]
    return array.at[tuple(index_at)].set(largest)


def setup_inputs(seed: int = 0) -> dict:
    keys = jax.random.split(jax.random.key(seed), 4)
    logits = draw_logits(jax.random.fold_in(keys[3], 71), 0)
    leaf_index = touch_ends(jax.random.randint(keys[1], (ROWS,), 0, LEAVES), jax.random.fold_in(keys[1], 1), 0, LEAVES - 1).astype(jnp.int32)
    labels = touch_ends(jax.random.randint(keys[2], (ROWS,), 0, C), jax.random.fold_in(keys[2], 1), 0, C - 1).astype(jnp.int32)
    return dict(logits=logits, leaf_index=leaf_index, labels=labels)


def block_terms(block_logits, block_leaf, block_label):
    peak = jnp.max(block_logits, axis=1, keepdims=True)
    expo = jnp.exp(block_logits - peak)
    total = jnp.sum(expo, axis=1, keepdims=True)
    prob = expo / total
    classes = jnp.arange(C, dtype=jnp.int32)[None, :]
    grad = prob - (block_label[:, None] == classes).astype(jnp.float32)
    hess = prob * (1.0 - prob)
    leaves = jnp.arange(LEAVES, dtype=jnp.int32)[None, :]
    onehot = (block_leaf[:, None] == leaves).astype(jnp.float32)
    dims = (((0,), (0,)), ((), ()))
    g_sum = lax.dot_general(onehot, grad, dims, precision=lax.Precision.HIGHEST, preferred_element_type=jnp.float32)
    h_sum = lax.dot_general(onehot, hess, dims, precision=lax.Precision.HIGHEST, preferred_element_type=jnp.float32)
    return g_sum, h_sum


def reference(logits, leaf_index, labels):
    blocks = logits.reshape(N_ROWS, ROW_DEV, C)
    leaf_blocks = leaf_index.reshape(N_ROWS, ROW_DEV)
    label_blocks = labels.reshape(N_ROWS, ROW_DEV)

    def step(carry, items):
        g_sum, h_sum = block_terms(items[0], items[1], items[2])
        return (carry[0] + g_sum, carry[1] + h_sum), None

    start = (jnp.zeros((LEAVES, C), jnp.float32), jnp.zeros((LEAVES, C), jnp.float32))
    sums, _ = lax.scan(step, start, (blocks, leaf_blocks, label_blocks))
    leaf_values = -0.3 * sums[0] / (sums[1] + 1.0)

    def apply(items):
        leaves = jnp.arange(LEAVES, dtype=jnp.int32)[None, :]
        onehot = (items[1][:, None] == leaves).astype(jnp.float32)
        return items[0] + jnp.dot(onehot, leaf_values, precision=lax.Precision.HIGHEST, preferred_element_type=jnp.float32)

    updated = lax.map(apply, (blocks, leaf_blocks)).reshape(ROWS, C)
    return leaf_values, updated
```

```python
import functools

import jax
import jax.numpy as jnp
from jax import lax
from jax.experimental import pallas as pl
from jax.experimental.pallas import tpu as pltpu
from jax.sharding import PartitionSpec as P

LEAVES = 128
LANE = 128
MIB = 2**20
F32 = jnp.float32
BF16 = jnp.bfloat16
IN_VMEM = pl.BlockSpec(memory_space=pltpu.VMEM)
IN_SMEM = pl.BlockSpec(memory_space=pltpu.SMEM)
IN_ANY = pl.BlockSpec(memory_space=pl.ANY)


def split(value):
    high = value.astype(BF16)
    return high, (value - high.astype(F32)).astype(BF16)


def params(limit):
    return pltpu.CompilerParams(vmem_limit_bytes=limit * MIB)


def stats_body(chunks, x_hbm, x_ref, e_ref, m_ref, s_ref, sems):
    step = x_hbm.shape[0] // chunks

    def fetch(i):
        at = pl.ds(i * step, step)
        return pltpu.make_async_copy(x_hbm.at[at], x_ref.at[at], sems.at[i])

    for i in range(chunks):
        fetch(i).start()
    diagonal = lax.broadcasted_iota(jnp.int32, (LANE, LANE), 0) == lax.broadcasted_iota(jnp.int32, (LANE, LANE), 1)
    for i in range(chunks):
        fetch(i).wait()
        for t in range(step // LANE):
            row = i * (step // LANE) + t
            at = pl.ds(row * LANE, LANE)
            x = x_ref[at]
            m = jnp.max(x, axis=1, keepdims=True)
            e = jnp.exp(x - m)
            s = jnp.sum(e, axis=1, keepdims=True)
            e_ref[at] = e
            m_ref[pl.ds(row, 1)] = jnp.sum(jnp.where(diagonal, m, 0.0), axis=0, keepdims=True)
            s_ref[pl.ds(row, 1)] = jnp.sum(jnp.where(diagonal, s, 0.0), axis=0, keepdims=True)


def local_stats(logits):
    rows, width = logits.shape
    chunks = 8
    full = pltpu.VMEM((rows, width), F32)
    small = jax.ShapeDtypeStruct((rows // LANE, LANE), F32)
    return pl.pallas_call(
        functools.partial(stats_body, chunks),
        out_shape=[full, full, small, small],
        in_specs=[IN_ANY],
        out_specs=[IN_VMEM] * 4,
        scratch_shapes=[pltpu.SemaphoreType.DMA((chunks,))],
        compiler_params=params(36),
        cost_estimate=pl.CostEstimate(flops=6 * rows * width, bytes_accessed=4 * rows * width, transcendentals=rows * width),
        name="local_stats",
    )(logits)


def index_body(offset_ref, leaf_ref, label_ref, cols_ref, rows_ref, class_ref):
    offset = offset_ref[0]
    sub = lax.broadcasted_iota(jnp.int32, (LANE, LANE), 0)
    lane = lax.broadcasted_iota(jnp.int32, (LANE, LANE), 1)
    for t in range(leaf_ref.shape[0]):
        at = pl.ds(t * LANE, LANE)
        leaf = jnp.broadcast_to(leaf_ref[pl.ds(t, 1)], (LANE, LANE))
        label = jnp.broadcast_to(label_ref[pl.ds(t, 1)] - offset, (LANE, LANE))
        cols_ref[:, at] = jnp.where(sub == leaf, 1.0, 0.0).astype(BF16)
        rows_ref[at] = jnp.where(lane == leaf.T, 1.0, 0.0).astype(BF16)
        class_ref[at] = label.T


def index_forms(offset, leaf_index, labels):
    rows = leaf_index.shape[0]
    shape = (rows // LANE, LANE)
    return pl.pallas_call(
        index_body,
        out_shape=[
            pltpu.VMEM((LEAVES, rows), BF16),
            pltpu.VMEM((rows, LEAVES), BF16),
            pltpu.VMEM((rows, LANE), jnp.int32),
        ],
        in_specs=[IN_SMEM, IN_VMEM, IN_VMEM],
        out_specs=[IN_VMEM] * 3,
        compiler_params=params(4),
        name="index_forms",
    )(offset, leaf_index.reshape(shape), labels.reshape(shape))


def sums_body(first, parties, block_ref, e_ref, hot_ref, class_ref, *refs):
    if first:
        peaks, totals = refs[:parties], refs[parties : 2 * parties]
        out_ref, scale_ref, acc_ref = refs[2 * parties :]
        peak = functools.reduce(jnp.maximum, [p[...] for p in peaks])
        grown = [jnp.exp(p[...] - peak) for p in peaks]
        total = functools.reduce(jnp.add, [g * t[...] for g, t in zip(grown, totals)])
        factor = grown[0] / total
    else:
        scale_ref, out_ref, acc_ref = refs
    start = pl.multiple_of(block_ref[0] * LANE, LANE)
    columns = pl.ds(start, LANE)
    step = 512
    own = lax.broadcasted_iota(jnp.int32, (step, LANE), 1) + start
    for i in range(e_ref.shape[0] // step):
        at = pl.ds(i * step, step)
        if first:
            for t in range(step // LANE):
                row = i * (step // LANE) + t
                scale_ref[pl.ds(row * LANE, LANE)] = jnp.broadcast_to(factor[row : row + 1], (LANE, LANE)).T
        prob = e_ref[at, columns] * scale_ref[at]
        grad = jnp.where(class_ref[at] == own, prob - 1.0, prob)
        hess = prob * (1.0 - prob)
        right = jnp.concatenate(split(grad) + split(hess), axis=1)
        part = jnp.dot(hot_ref[:, at], right, preferred_element_type=F32)
        if i == 0:
            acc_ref[...] = part
        else:
            acc_ref[...] += part
    out_ref[:LEAVES] = acc_ref[:, :LANE] + acc_ref[:, LANE : 2 * LANE]
    out_ref[LEAVES:] = acc_ref[:, 2 * LANE : 3 * LANE] + acc_ref[:, 3 * LANE :]


def leaf_sums(block, e, hot, classes, scale=None, stats=None):
    rows = e.shape[0]
    first = scale is None
    out = [jax.ShapeDtypeStruct((2 * LEAVES, LANE), F32)]
    if first:
        out.append(pltpu.VMEM((rows, LANE), F32))
        more = [s[0] for s in stats] + [s[1] for s in stats]
    else:
        more = [scale]
    got = pl.pallas_call(
        functools.partial(sums_body, first, len(more) // 2),
        out_shape=out,
        in_specs=[IN_SMEM] + [IN_VMEM] * (3 + len(more)),
        out_specs=[IN_VMEM] * len(out),
        scratch_shapes=[pltpu.VMEM((LEAVES, 4 * LANE), F32)],
        compiler_params=params(6),
        cost_estimate=pl.CostEstimate(flops=8 * rows * LEAVES * LANE, bytes_accessed=8 * rows * LANE, transcendentals=0),
        name="leaf_sums",
    )(block, e, hot, classes, *more)
    return got if first else got[0]


def apply_body(first, chunks, block_ref, value_ref, x_ref, hot_ref, *refs):
    if not first:
        refs = refs[2:]
    value_hbm, updated_hbm, tile_ref, sems = refs
    columns = pl.ds(pl.multiple_of(block_ref[0] * LANE, LANE), LANE)
    step = x_ref.shape[0] // chunks

    def send(i):
        at = pl.ds(i * step, step)
        return pltpu.make_async_copy(tile_ref.at[at], updated_hbm.at[at, columns], sems.at[i])

    value_copy = pltpu.make_async_copy(value_ref, value_hbm.at[:, columns], sems.at[chunks])
    value_copy.start()
    right = jnp.concatenate(split(value_ref[...]), axis=0)
    for i in range(chunks):
        at = pl.ds(i * step, step)
        hot = hot_ref[at]
        left = jnp.concatenate([hot, hot], axis=1)
        tile_ref[at] = x_ref[at, columns] + jnp.dot(left, right, preferred_element_type=F32)
        send(i).start()
    for i in range(chunks):
        send(i).wait()
    value_copy.wait()


def apply_block(block, value, x, hot, held=None):
    rows, width = x.shape
    chunks = 8
    first = held is None
    more = [] if first else list(held)
    return pl.pallas_call(
        functools.partial(apply_body, first, chunks),
        out_shape=[jax.ShapeDtypeStruct((LEAVES, width), F32), jax.ShapeDtypeStruct((rows, width), F32)],
        in_specs=[IN_SMEM] + [IN_VMEM] * 3 + [IN_ANY] * len(more),
        out_specs=[IN_ANY] * 2,
        scratch_shapes=[pltpu.VMEM((rows, LANE), F32), pltpu.SemaphoreType.DMA((chunks + 1,))],
        input_output_aliases={} if first else {4: 0, 5: 1},
        compiler_params=params(6),
        cost_estimate=pl.CostEstimate(flops=4 * rows * LEAVES * LANE, bytes_accessed=8 * rows * LANE, transcendentals=0),
        name="apply_block",
    )(block, value, x, hot, *more)


def newton(sums):
    return -0.3 * sums[:LEAVES] / (sums[LEAVES:] + 1.0)


def per_device(n_rows, n_cls, logits, leaf_index, labels):
    width = logits.shape[1]
    blocks = width // LANE
    me = lax.axis_index("rows").astype(jnp.int32)
    offset = (lax.axis_index("cls") * width).astype(jnp.int32).reshape(1)

    def swap(value, bit):
        return lax.ppermute(value, "rows", [(i, i ^ bit) for i in range(n_rows)])

    x, e, peak, total = local_stats(logits)
    mine = jnp.stack([peak, total])
    stats = [mine]
    for shift in range(1, n_cls):
        stats.append(lax.ppermute(mine, "cls", [(i, (i + shift) % n_cls) for i in range(n_cls)]))
    hot_cols, hot_rows, classes = index_forms(offset, leaf_index, labels)

    planes = n_rows == 16 and blocks == 4
    order = [1, 3, 2, 0] if planes else list(range(blocks))
    where = [((me & 3) ^ d).reshape(1) if planes else jnp.full((1,), d, jnp.int32) for d in order]
    scale = None
    parts = []
    for block in where:
        if scale is None:
            part, scale = leaf_sums(block, e, hot_cols, classes, stats=stats)
        else:
            part = leaf_sums(block, e, hot_cols, classes, scale=scale)
        parts.append(part)

    if planes:
        got = [swap(part, d) for part, d in zip(parts[:3], order[:3])]
        sums = parts[3] + got[0] + got[1] + got[2]
        sums = sums + swap(sums, 4)
        sums = sums + swap(sums, 8)
        value = newton(sums)
        values = [(where[3], value)] + [(w, swap(value, d)) for w, d in zip(where[:3], order[:3])]
    else:
        values = list(zip(where, [newton(s) for s in lax.psum(parts, "rows")]))

    held = None
    for block, value in values:
        held = apply_block(block, value, x, hot_rows, held)
    return held[0], held[1]


def solution(mesh):
    return jax.shard_map(
        functools.partial(per_device, mesh.shape["rows"], mesh.shape["cls"]),
        mesh=mesh,
        in_specs=(P("rows", "cls"), P("rows"), P("rows")),
        out_specs=(P(None, "cls"), P("rows", "cls")),
        check_vma=False,
    )
```

```python
import functools

import jax
import jax.numpy as jnp
from jax import lax
from jax.experimental import pallas as pl
from jax.experimental.pallas import tpu as pltpu
from jax.sharding import PartitionSpec as P

LEAVES = 128
LANE = 128
MIB = 2**20
F32 = jnp.float32
BF16 = jnp.bfloat16
IN_VMEM = pl.BlockSpec(memory_space=pltpu.VMEM)
IN_ANY = pl.BlockSpec(memory_space=pl.ANY)


def split(value):
    high = value.astype(BF16)
    return high, (value - high.astype(F32)).astype(BF16)


def params(limit):
    return pltpu.CompilerParams(vmem_limit_bytes=limit * MIB)


def stats_body(chunks, x_hbm, x_ref, e_ref, m_ref, s_ref, sems):
    step = x_hbm.shape[0] // chunks

    def fetch(i):
        at = pl.ds(i * step, step)
        return pltpu.make_async_copy(x_hbm.at[at], x_ref.at[at], sems.at[i])

    for i in range(chunks):
        fetch(i).start()
    diagonal = lax.broadcasted_iota(jnp.int32, (LANE, LANE), 0) == lax.broadcasted_iota(jnp.int32, (LANE, LANE), 1)
    for i in range(chunks):
        fetch(i).wait()
        for t in range(step // LANE):
            row = i * (step // LANE) + t
            at = pl.ds(row * LANE, LANE)
            x = x_ref[at]
            m = jnp.max(x, axis=1, keepdims=True)
            e = jnp.exp(x - m)
            s = jnp.sum(e, axis=1, keepdims=True)
            e_ref[at] = e
            m_ref[pl.ds(row, 1)] = jnp.sum(jnp.where(diagonal, m, 0.0), axis=0, keepdims=True)
            s_ref[pl.ds(row, 1)] = jnp.sum(jnp.where(diagonal, s, 0.0), axis=0, keepdims=True)


def local_stats(logits):
    rows, width = logits.shape
    chunks = 8
    full = pltpu.VMEM((rows, width), F32)
    small = jax.ShapeDtypeStruct((rows // LANE, LANE), F32)
    return pl.pallas_call(
        functools.partial(stats_body, chunks),
        out_shape=[full, full, small, small],
        in_specs=[IN_ANY],
        out_specs=[IN_VMEM] * 4,
        scratch_shapes=[pltpu.SemaphoreType.DMA((chunks,))],
        compiler_params=params(36),
        cost_estimate=pl.CostEstimate(flops=6 * rows * width, bytes_accessed=4 * rows * width, transcendentals=rows * width),
        name="local_stats",
    )(logits)


def index_body(width, leaf_ref, label_ref, cols_ref, rows_ref, class_ref):
    offset = lax.axis_index("cls") * width
    sub = lax.broadcasted_iota(jnp.int32, (LANE, LANE), 0)
    lane = lax.broadcasted_iota(jnp.int32, (LANE, LANE), 1)
    for t in range(leaf_ref.shape[0]):
        at = pl.ds(t * LANE, LANE)
        leaf = jnp.broadcast_to(leaf_ref[pl.ds(t, 1)], (LANE, LANE))
        label = jnp.broadcast_to(label_ref[pl.ds(t, 1)] - offset, (LANE, LANE))
        cols_ref[:, at] = jnp.where(sub == leaf, 1.0, 0.0).astype(BF16)
        rows_ref[at] = jnp.where(lane == leaf.T, 1.0, 0.0).astype(BF16)
        class_ref[at] = label.T


def index_forms(width, leaf_index, labels):
    rows = leaf_index.shape[0]
    shape = (rows // LANE, LANE)
    return pl.pallas_call(
        functools.partial(index_body, width),
        out_shape=[
            pltpu.VMEM((LEAVES, rows), BF16),
            pltpu.VMEM((rows, LEAVES), BF16),
            pltpu.VMEM((rows, LANE), jnp.int32),
        ],
        in_specs=[IN_VMEM, IN_VMEM],
        out_specs=[IN_VMEM] * 3,
        compiler_params=params(4),
        name="index_forms",
    )(leaf_index.reshape(shape), labels.reshape(shape))


def block_start(planes, block):
    if planes:
        block = (lax.axis_index("rows") & 3) ^ block
        return pl.multiple_of(block * LANE, LANE)
    return block * LANE


def sums_body(first, parties, place, e_ref, hot_ref, class_ref, *refs):
    if first:
        peaks, totals = refs[:parties], refs[parties : 2 * parties]
        out_ref, scale_ref, acc_ref = refs[2 * parties :]
        peak = functools.reduce(jnp.maximum, [p[...] for p in peaks])
        grown = [jnp.exp(p[...] - peak) for p in peaks]
        total = functools.reduce(jnp.add, [g * t[...] for g, t in zip(grown, totals)])
        factor = grown[0] / total
    else:
        scale_ref, out_ref, acc_ref = refs
    start = block_start(*place)
    columns = pl.ds(start, LANE)
    step = 512
    own = lax.broadcasted_iota(jnp.int32, (step, LANE), 1) + start
    for i in range(e_ref.shape[0] // step):
        at = pl.ds(i * step, step)
        if first:
            for t in range(step // LANE):
                row = i * (step // LANE) + t
                scale_ref[pl.ds(row * LANE, LANE)] = jnp.broadcast_to(factor[row : row + 1], (LANE, LANE)).T
        prob = e_ref[at, columns] * scale_ref[at]
        grad = jnp.where(class_ref[at] == own, prob - 1.0, prob)
        hess = prob * (1.0 - prob)
        right = jnp.concatenate(split(grad) + split(hess), axis=1)
        part = jnp.dot(hot_ref[:, at], right, preferred_element_type=F32)
        if i == 0:
            acc_ref[...] = part
        else:
            acc_ref[...] += part
    out_ref[:LEAVES] = acc_ref[:, :LANE] + acc_ref[:, LANE : 2 * LANE]
    out_ref[LEAVES:] = acc_ref[:, 2 * LANE : 3 * LANE] + acc_ref[:, 3 * LANE :]


def leaf_sums(place, e, hot, classes, scale=None, stats=None):
    rows = e.shape[0]
    first = scale is None
    out = [jax.ShapeDtypeStruct((2 * LEAVES, LANE), F32)]
    if first:
        out.append(pltpu.VMEM((rows, LANE), F32))
        more = [s[0] for s in stats] + [s[1] for s in stats]
    else:
        more = [scale]
    got = pl.pallas_call(
        functools.partial(sums_body, first, len(more) // 2, place),
        out_shape=out,
        in_specs=[IN_VMEM] * (3 + len(more)),
        out_specs=[IN_VMEM] * len(out),
        scratch_shapes=[pltpu.VMEM((LEAVES, 4 * LANE), F32)],
        compiler_params=params(6),
        cost_estimate=pl.CostEstimate(flops=8 * rows * LEAVES * LANE, bytes_accessed=8 * rows * LANE, transcendentals=0),
        name="leaf_sums",
    )(e, hot, classes, *more)
    return got if first else got[0]


def apply_body(first, chunks, place, value_ref, x_ref, hot_ref, *refs):
    if not first:
        refs = refs[2:]
    value_hbm, updated_hbm, tile_ref, sems = refs
    columns = pl.ds(block_start(*place), LANE)
    step = x_ref.shape[0] // chunks

    def send(i):
        at = pl.ds(i * step, step)
        return pltpu.make_async_copy(tile_ref.at[at], updated_hbm.at[at, columns], sems.at[i])

    value_copy = pltpu.make_async_copy(value_ref, value_hbm.at[:, columns], sems.at[chunks])
    value_copy.start()
    right = jnp.concatenate(split(value_ref[...]), axis=0)
    for i in range(chunks):
        at = pl.ds(i * step, step)
        hot = hot_ref[at]
        left = jnp.concatenate([hot, hot], axis=1)
        tile_ref[at] = x_ref[at, columns] + jnp.dot(left, right, preferred_element_type=F32)
        send(i).start()
    for i in range(chunks):
        send(i).wait()
    value_copy.wait()


def apply_block(place, value, x, hot, held=None):
    rows, width = x.shape
    chunks = 8
    first = held is None
    more = [] if first else list(held)
    return pl.pallas_call(
        functools.partial(apply_body, first, chunks, place),
        out_shape=[jax.ShapeDtypeStruct((LEAVES, width), F32), jax.ShapeDtypeStruct((rows, width), F32)],
        in_specs=[IN_VMEM] * 3 + [IN_ANY] * len(more),
        out_specs=[IN_ANY] * 2,
        scratch_shapes=[pltpu.VMEM((rows, LANE), F32), pltpu.SemaphoreType.DMA((chunks + 1,))],
        input_output_aliases={} if first else {3: 0, 4: 1},
        compiler_params=params(6),
        cost_estimate=pl.CostEstimate(flops=4 * rows * LEAVES * LANE, bytes_accessed=8 * rows * LANE, transcendentals=0),
        name="apply_block",
    )(value, x, hot, *more)


def newton(sums):
    return -0.3 * sums[:LEAVES] / (sums[LEAVES:] + 1.0)


def per_device(n_rows, n_cls, logits, leaf_index, labels):
    width = logits.shape[1]
    blocks = width // LANE

    def swap(value, bit):
        return lax.ppermute(value, "rows", [(i, i ^ bit) for i in range(n_rows)])

    x, e, peak, total = local_stats(logits)
    mine = jnp.stack([peak, total])
    stats = [mine]
    for shift in range(1, n_cls):
        stats.append(lax.ppermute(mine, "cls", [(i, (i + shift) % n_cls) for i in range(n_cls)]))
    hot_cols, hot_rows, classes = index_forms(width, leaf_index, labels)

    planes = n_rows == 16 and blocks == 4
    order = [1, 3, 2, 0] if planes else list(range(blocks))
    where = [(planes, d) for d in order]
    scale = None
    parts = []
    for block in where:
        if scale is None:
            part, scale = leaf_sums(block, e, hot_cols, classes, stats=stats)
        else:
            part = leaf_sums(block, e, hot_cols, classes, scale=scale)
        parts.append(part)

    if planes:
        got = [swap(part, d) for part, d in zip(parts[:3], order[:3])]
        sums = parts[3] + got[0] + got[1] + got[2]
        sums = sums + swap(sums, 4)
        sums = sums + swap(sums, 8)
        value = newton(sums)
        values = [(where[3], value)] + [(w, swap(value, d)) for w, d in zip(where[:3], order[:3])]
    else:
        values = list(zip(where, [newton(s) for s in lax.psum(parts, "rows")]))

    held = None
    for block, value in values:
        held = apply_block(block, value, x, hot_rows, held)
    return held[0], held[1]


def solution(mesh):
    return jax.shard_map(
        functools.partial(per_device, mesh.shape["rows"], mesh.shape["cls"]),
        mesh=mesh,
        in_specs=(P("rows", "cls"), P("rows"), P("rows")),
        out_specs=(P(None, "cls"), P("rows", "cls")),
        check_vma=False,
    )
```

```python
import functools

import jax
import jax.numpy as jnp
from jax import lax
from jax.experimental import pallas as pl
from jax.experimental.pallas import tpu as pltpu
from jax.sharding import PartitionSpec as P

LEAVES = 128
LANE = 128
MIB = 2**20
F32 = jnp.float32
BF16 = jnp.bfloat16
IN_VMEM = pl.BlockSpec(memory_space=pltpu.VMEM)
IN_ANY = pl.BlockSpec(memory_space=pl.ANY)


def split(value):
    high = value.astype(BF16)
    return high, (value - high.astype(F32)).astype(BF16)


def params(limit):
    return pltpu.CompilerParams(vmem_limit_bytes=limit * MIB)


def stats_body(chunks, x_hbm, x_ref, e_ref, m_ref, s_ref, sems):
    step = x_hbm.shape[0] // chunks

    def fetch(i):
        at = pl.ds(i * step, step)
        return pltpu.make_async_copy(x_hbm.at[at], x_ref.at[at], sems.at[i])

    for i in range(chunks):
        fetch(i).start()
    diagonal = lax.broadcasted_iota(jnp.int32, (LANE, LANE), 0) == lax.broadcasted_iota(jnp.int32, (LANE, LANE), 1)
    for i in range(chunks):
        fetch(i).wait()
        for t in range(step // LANE):
            row = i * (step // LANE) + t
            at = pl.ds(row * LANE, LANE)
            x = x_ref[at]
            m = jnp.max(x, axis=1, keepdims=True)
            e = jnp.exp(x - m)
            s = jnp.sum(e, axis=1, keepdims=True)
            e_ref[at] = e
            m_ref[pl.ds(row, 1)] = jnp.sum(jnp.where(diagonal, m, 0.0), axis=0, keepdims=True)
            s_ref[pl.ds(row, 1)] = jnp.sum(jnp.where(diagonal, s, 0.0), axis=0, keepdims=True)


def local_stats(logits):
    rows, width = logits.shape
    chunks = 8
    full = pltpu.VMEM((rows, width), F32)
    small = jax.ShapeDtypeStruct((rows // LANE, LANE), F32)
    return pl.pallas_call(
        functools.partial(stats_body, chunks),
        out_shape=[full, full, small, small],
        in_specs=[IN_ANY],
        out_specs=[IN_VMEM] * 4,
        scratch_shapes=[pltpu.SemaphoreType.DMA((chunks,))],
        compiler_params=params(36),
        cost_estimate=pl.CostEstimate(flops=6 * rows * width, bytes_accessed=4 * rows * width, transcendentals=rows * width),
        name="local_stats",
    )(logits)


def index_body(width, leaf_ref, label_ref, cols_ref, rows_ref, class_ref):
    offset = lax.axis_index("cls") * width
    sub = lax.broadcasted_iota(jnp.int32, (LANE, LANE), 0)
    lane = lax.broadcasted_iota(jnp.int32, (LANE, LANE), 1)
    for t in range(leaf_ref.shape[0]):
        at = pl.ds(t * LANE, LANE)
        leaf = jnp.broadcast_to(leaf_ref[pl.ds(t, 1)], (LANE, LANE))
        label = jnp.broadcast_to(label_ref[pl.ds(t, 1)] - offset, (LANE, LANE))
        cols_ref[:, at] = jnp.where(sub == leaf, 1.0, 0.0).astype(BF16)
        rows_ref[at] = jnp.where(lane == leaf.T, 1.0, 0.0).astype(BF16)
        class_ref[at] = label.T


def index_forms(width, leaf_index, labels):
    rows = leaf_index.shape[0]
    shape = (rows // LANE, LANE)
    return pl.pallas_call(
        functools.partial(index_body, width),
        out_shape=[
            pltpu.VMEM((LEAVES, rows), BF16),
            pltpu.VMEM((rows, LEAVES), BF16),
            pltpu.VMEM((rows, LANE), jnp.int32),
        ],
        in_specs=[IN_VMEM, IN_VMEM],
        out_specs=[IN_VMEM] * 3,
        compiler_params=params(4),
        name="index_forms",
    )(leaf_index.reshape(shape), labels.reshape(shape))


def block_start(planes, block):
    if planes:
        block = (lax.axis_index("rows") & 3) ^ block
        return pl.multiple_of(block * LANE, LANE)
    return block * LANE


def sums_body(first, parties, place, e_ref, hot_ref, class_ref, *refs):
    if first:
        peaks, totals = refs[:parties], refs[parties : 2 * parties]
        out_ref, scale_ref, acc_ref = refs[2 * parties :]
        peak = functools.reduce(jnp.maximum, [p[...] for p in peaks])
        grown = [jnp.exp(p[...] - peak) for p in peaks]
        total = functools.reduce(jnp.add, [g * t[...] for g, t in zip(grown, totals)])
        factor = grown[0] / total
    else:
        scale_ref, _, out_ref, acc_ref = refs
    start = block_start(*place)
    columns = pl.ds(start, LANE)
    step = 512
    own = lax.broadcasted_iota(jnp.int32, (step, LANE), 1) + start
    for i in range(e_ref.shape[0] // step):
        at = pl.ds(i * step, step)
        if first:
            for t in range(step // LANE):
                row = i * (step // LANE) + t
                scale_ref[pl.ds(row * LANE, LANE)] = jnp.broadcast_to(factor[row : row + 1], (LANE, LANE)).T
        prob = e_ref[at, columns] * scale_ref[at]
        grad = jnp.where(class_ref[at] == own, prob - 1.0, prob)
        hess = prob * (1.0 - prob)
        right = jnp.concatenate(split(grad) + split(hess), axis=1)
        part = jnp.dot(hot_ref[:, at], right, preferred_element_type=F32)
        if i == 0:
            acc_ref[...] = part
        else:
            acc_ref[...] += part
    out_ref[:LEAVES] = acc_ref[:, :LANE] + acc_ref[:, LANE : 2 * LANE]
    out_ref[LEAVES:] = acc_ref[:, 2 * LANE : 3 * LANE] + acc_ref[:, 3 * LANE :]


def leaf_sums(place, e, hot, classes, scale=None, stats=None, after=None):
    rows = e.shape[0]
    first = scale is None
    out = [jax.ShapeDtypeStruct((2 * LEAVES, LANE), F32)]
    if first:
        out.append(pltpu.VMEM((rows, LANE), F32))
        more = [s[0] for s in stats] + [s[1] for s in stats]
    else:
        more = [scale, after]
    got = pl.pallas_call(
        functools.partial(sums_body, first, len(more) // 2, place),
        out_shape=out,
        in_specs=[IN_VMEM] * (3 + len(more)),
        out_specs=[IN_VMEM] * len(out),
        scratch_shapes=[pltpu.VMEM((LEAVES, 4 * LANE), F32)],
        compiler_params=params(6),
        cost_estimate=pl.CostEstimate(flops=1, bytes_accessed=1, transcendentals=0),
        name="leaf_sums",
    )(e, hot, classes, *more)
    return got if first else got[0]


def apply_body(first, chunks, places, x_ref, hot_ref, *refs):
    count = len(places)
    values, refs = refs[:count], refs[count:]
    if not first:
        refs = refs[2:]
    value_hbm, updated_hbm, tile_ref, sems, value_sems = refs
    columns = [pl.ds(block_start(*place), LANE) for place in places]
    step = x_ref.shape[0] // chunks

    def send(i, b):
        at = pl.ds(i * step, step)
        return pltpu.make_async_copy(tile_ref.at[b, at], updated_hbm.at[at, columns[b]], sems.at[i, b])

    def send_value(b):
        return pltpu.make_async_copy(values[b], value_hbm.at[:, columns[b]], value_sems.at[b])

    for b in range(count):
        send_value(b).start()
    right = [jnp.concatenate(split(value[...]), axis=0) for value in values]
    for i in range(chunks):
        at = pl.ds(i * step, step)
        hot = hot_ref[at]
        left = jnp.concatenate([hot, hot], axis=1)
        for b in range(count):
            tile_ref[b, at] = x_ref[at, columns[b]] + jnp.dot(left, right[b], preferred_element_type=F32)
            send(i, b).start()
    for i in range(chunks):
        for b in range(count):
            send(i, b).wait()
    for b in range(count):
        send_value(b).wait()


def apply_blocks(places, values, x, hot, held=None):
    rows, width = x.shape
    chunks, count = 8, len(places)
    first = held is None
    more = [] if first else list(held)
    return pl.pallas_call(
        functools.partial(apply_body, first, chunks, places),
        out_shape=[jax.ShapeDtypeStruct((LEAVES, width), F32), jax.ShapeDtypeStruct((rows, width), F32)],
        in_specs=[IN_VMEM] * (2 + count) + [IN_ANY] * len(more),
        out_specs=[IN_ANY] * 2,
        scratch_shapes=[
            pltpu.VMEM((count, rows, LANE), F32),
            pltpu.SemaphoreType.DMA((chunks, count)),
            pltpu.SemaphoreType.DMA((count,)),
        ],
        input_output_aliases={} if first else {2 + count: 0, 3 + count: 1},
        compiler_params=params(4 + 3 * count),
        cost_estimate=pl.CostEstimate(
            flops=4 * count * rows * LEAVES * LANE, bytes_accessed=4 * count * rows * LANE, transcendentals=0
        ),
        name="apply_blocks",
    )(x, hot, *values, *more)


def newton(sums):
    return -0.3 * sums[:LEAVES] / (sums[LEAVES:] + 1.0)


def per_device(n_rows, n_cls, logits, leaf_index, labels):
    width = logits.shape[1]
    blocks = width // LANE

    def swap(value, bit):
        return lax.ppermute(value, "rows", [(i, i ^ bit) for i in range(n_rows)])

    x, e, peak, total = local_stats(logits)
    mine = jnp.stack([peak, total])
    stats = [mine]
    for shift in range(1, n_cls):
        stats.append(lax.ppermute(mine, "cls", [(i, (i + shift) % n_cls) for i in range(n_cls)]))
    hot_cols, hot_rows, classes = index_forms(width, leaf_index, labels)

    planes = n_rows == 16 and blocks == 4
    order = [3, 1, 2, 0] if planes else list(range(blocks))
    where = [(planes, d) for d in order]
    scale = None
    parts = []
    for block in where:
        if scale is None:
            part, scale = leaf_sums(block, e, hot_cols, classes, stats=stats)
        else:
            part = leaf_sums(block, e, hot_cols, classes, scale=scale, after=parts[-1])
        parts.append(part)

    if planes:
        got = [swap(part, d) for part, d in zip(parts[:3], order[:3])]
        sums = parts[3]
        for part in got:
            sums = lax.optimization_barrier(sums + part)
        sums = sums + swap(sums, 4)
        sums = sums + swap(sums, 8)
        value = newton(sums)
        values = [swap(value, d) for d in order[:3]] + [value]
    else:
        values = [newton(s) for s in lax.psum(parts, "rows")]

    if planes:
        held = apply_blocks(where[3:], values[3:], x, hot_rows)
        held = apply_blocks(where[:1], values[:1], x, hot_rows, held)
        held = apply_blocks(where[1:3], values[1:3], x, hot_rows, held)
    else:
        held = apply_blocks(where, values, x, hot_rows)
    return held[0], held[1]


def solution(mesh):
    return jax.shard_map(
        functools.partial(per_device, mesh.shape["rows"], mesh.shape["cls"]),
        mesh=mesh,
        in_specs=(P("rows", "cls"), P("rows"), P("rows")),
        out_specs=(P(None, "cls"), P("rows", "cls")),
        check_vma=False,
    )
```

```python
import functools

import jax
import jax.numpy as jnp
from jax import lax
from jax.experimental import pallas as pl
from jax.experimental.pallas import tpu as pltpu
from jax.sharding import PartitionSpec as P

LEAVES = 128
LANE = 128
MIB = 2**20
F32 = jnp.float32
BF16 = jnp.bfloat16
IN_VMEM = pl.BlockSpec(memory_space=pltpu.VMEM)
IN_ANY = pl.BlockSpec(memory_space=pl.ANY)


def split(value):
    high = value.astype(BF16)
    return high, (value - high.astype(F32)).astype(BF16)


def params(limit):
    return pltpu.CompilerParams(vmem_limit_bytes=limit * MIB)


def stats_body(chunks, x_hbm, x_ref, e_ref, m_ref, s_ref, sems):
    step = x_hbm.shape[0] // chunks

    def fetch(i):
        at = pl.ds(i * step, step)
        return pltpu.make_async_copy(x_hbm.at[at], x_ref.at[at], sems.at[i])

    for i in range(chunks):
        fetch(i).start()
    diagonal = lax.broadcasted_iota(jnp.int32, (LANE, LANE), 0) == lax.broadcasted_iota(jnp.int32, (LANE, LANE), 1)
    for i in range(chunks):
        fetch(i).wait()
        for t in range(step // LANE):
            row = i * (step // LANE) + t
            at = pl.ds(row * LANE, LANE)
            x = x_ref[at]
            m = jnp.max(x, axis=1, keepdims=True)
            e = jnp.exp(x - m)
            s = jnp.sum(e, axis=1, keepdims=True)
            e_ref[at] = e
            m_ref[pl.ds(row, 1)] = jnp.sum(jnp.where(diagonal, m, 0.0), axis=0, keepdims=True)
            s_ref[pl.ds(row, 1)] = jnp.sum(jnp.where(diagonal, s, 0.0), axis=0, keepdims=True)


def local_stats(logits):
    rows, width = logits.shape
    chunks = 8
    full = pltpu.VMEM((rows, width), F32)
    small = jax.ShapeDtypeStruct((rows // LANE, LANE), F32)
    return pl.pallas_call(
        functools.partial(stats_body, chunks),
        out_shape=[full, full, small, small],
        in_specs=[IN_ANY],
        out_specs=[IN_VMEM] * 4,
        scratch_shapes=[pltpu.SemaphoreType.DMA((chunks,))],
        compiler_params=params(36),
        cost_estimate=pl.CostEstimate(flops=6 * rows * width, bytes_accessed=4 * rows * width, transcendentals=rows * width),
        name="local_stats",
    )(logits)


def index_body(width, leaf_ref, label_ref, cols_ref, rows_ref, class_ref):
    offset = lax.axis_index("cls") * width
    sub = lax.broadcasted_iota(jnp.int32, (LANE, LANE), 0)
    lane = lax.broadcasted_iota(jnp.int32, (LANE, LANE), 1)
    for t in range(leaf_ref.shape[0]):
        at = pl.ds(t * LANE, LANE)
        leaf = jnp.broadcast_to(leaf_ref[pl.ds(t, 1)], (LANE, LANE))
        label = jnp.broadcast_to(label_ref[pl.ds(t, 1)] - offset, (LANE, LANE))
        cols_ref[:, at] = jnp.where(sub == leaf, 1.0, 0.0).astype(BF16)
        rows_ref[at] = jnp.where(lane == leaf.T, 1.0, 0.0).astype(BF16)
        class_ref[at] = label.T


def index_forms(width, leaf_index, labels):
    rows = leaf_index.shape[0]
    shape = (rows // LANE, LANE)
    return pl.pallas_call(
        functools.partial(index_body, width),
        out_shape=[
            pltpu.VMEM((LEAVES, rows), BF16),
            pltpu.VMEM((rows, LEAVES), BF16),
            pltpu.VMEM((rows, LANE), jnp.int32),
        ],
        in_specs=[IN_VMEM, IN_VMEM],
        out_specs=[IN_VMEM] * 3,
        compiler_params=params(4),
        name="index_forms",
    )(leaf_index.reshape(shape), labels.reshape(shape))


def block_start(planes, block):
    if planes:
        far = jnp.where(lax.axis_index("cls") == 0, *block)
        return pl.multiple_of(((lax.axis_index("rows") & 3) ^ far) * LANE, LANE)
    return block * LANE


def sums_body(first, parties, place, e_ref, hot_ref, class_ref, *refs):
    if first:
        peaks, totals = refs[:parties], refs[parties : 2 * parties]
        out_ref, scale_ref, acc_ref = refs[2 * parties :]
        peak = functools.reduce(jnp.maximum, [p[...] for p in peaks])
        grown = [jnp.exp(p[...] - peak) for p in peaks]
        total = functools.reduce(jnp.add, [g * t[...] for g, t in zip(grown, totals)])
        factor = grown[0] / total
    else:
        scale_ref, _, out_ref, acc_ref = refs
    start = block_start(*place)
    columns = pl.ds(start, LANE)
    step = 512
    own = lax.broadcasted_iota(jnp.int32, (step, LANE), 1) + start
    for i in range(e_ref.shape[0] // step):
        at = pl.ds(i * step, step)
        if first:
            for t in range(step // LANE):
                row = i * (step // LANE) + t
                scale_ref[pl.ds(row * LANE, LANE)] = jnp.broadcast_to(factor[row : row + 1], (LANE, LANE)).T
        prob = e_ref[at, columns] * scale_ref[at]
        grad = jnp.where(class_ref[at] == own, prob - 1.0, prob)
        hess = prob * (1.0 - prob)
        right = jnp.concatenate(split(grad) + split(hess), axis=1)
        part = jnp.dot(hot_ref[:, at], right, preferred_element_type=F32)
        if i == 0:
            acc_ref[...] = part
        else:
            acc_ref[...] += part
    out_ref[:LEAVES] = acc_ref[:, :LANE] + acc_ref[:, LANE : 2 * LANE]
    out_ref[LEAVES:] = acc_ref[:, 2 * LANE : 3 * LANE] + acc_ref[:, 3 * LANE :]


def leaf_sums(place, e, hot, classes, scale=None, stats=None, after=None):
    rows = e.shape[0]
    first = scale is None
    out = [jax.ShapeDtypeStruct((2 * LEAVES, LANE), F32)]
    if first:
        out.append(pltpu.VMEM((rows, LANE), F32))
        more = [s[0] for s in stats] + [s[1] for s in stats]
    else:
        more = [scale, after]
    got = pl.pallas_call(
        functools.partial(sums_body, first, len(more) // 2, place),
        out_shape=out,
        in_specs=[IN_VMEM] * (3 + len(more)),
        out_specs=[IN_VMEM] * len(out),
        scratch_shapes=[pltpu.VMEM((LEAVES, 4 * LANE), F32)],
        compiler_params=params(6),
        cost_estimate=pl.CostEstimate(flops=1, bytes_accessed=1, transcendentals=0),
        name="leaf_sums",
    )(e, hot, classes, *more)
    return got if first else got[0]


def apply_body(first, chunks, places, x_ref, hot_ref, *refs):
    count = len(places)
    values, refs = refs[:count], refs[count:]
    if not first:
        refs = refs[2:]
    value_hbm, updated_hbm, tile_ref, sems, value_sems = refs
    columns = [pl.ds(block_start(*place), LANE) for place in places]
    step = x_ref.shape[0] // chunks

    def send(i, b):
        at = pl.ds(i * step, step)
        return pltpu.make_async_copy(tile_ref.at[b, at], updated_hbm.at[at, columns[b]], sems.at[i, b])

    def send_value(b):
        return pltpu.make_async_copy(values[b], value_hbm.at[:, columns[b]], value_sems.at[b])

    for b in range(count):
        send_value(b).start()
    right = [jnp.concatenate(split(value[...]), axis=0) for value in values]
    for i in range(chunks):
        at = pl.ds(i * step, step)
        hot = hot_ref[at]
        left = jnp.concatenate([hot, hot], axis=1)
        for b in range(count):
            tile_ref[b, at] = x_ref[at, columns[b]] + jnp.dot(left, right[b], preferred_element_type=F32)
            send(i, b).start()
    for i in range(chunks):
        for b in range(count):
            send(i, b).wait()
    for b in range(count):
        send_value(b).wait()


def apply_blocks(places, values, x, hot, held=None):
    rows, width = x.shape
    chunks, count = 8, len(places)
    first = held is None
    more = [] if first else list(held)
    return pl.pallas_call(
        functools.partial(apply_body, first, chunks, places),
        out_shape=[jax.ShapeDtypeStruct((LEAVES, width), F32), jax.ShapeDtypeStruct((rows, width), F32)],
        in_specs=[IN_VMEM] * (2 + count) + [IN_ANY] * len(more),
        out_specs=[IN_ANY] * 2,
        scratch_shapes=[
            pltpu.VMEM((count, rows, LANE), F32),
            pltpu.SemaphoreType.DMA((chunks, count)),
            pltpu.SemaphoreType.DMA((count,)),
        ],
        input_output_aliases={} if first else {2 + count: 0, 3 + count: 1},
        compiler_params=params(4 + 3 * count),
        cost_estimate=pl.CostEstimate(
            flops=4 * count * rows * LEAVES * LANE, bytes_accessed=4 * count * rows * LANE, transcendentals=0
        ),
        name="apply_blocks",
    )(x, hot, *values, *more)


def newton(sums):
    return -0.3 * sums[:LEAVES] / (sums[LEAVES:] + 1.0)


def per_device(n_rows, n_cls, logits, leaf_index, labels):
    width = logits.shape[1]
    blocks = width // LANE

    def swap(value, far):
        pairs = [(row * n_cls + core, (row ^ far[core]) * n_cls + core) for row in range(n_rows) for core in range(n_cls)]
        return lax.ppermute(value, ("rows", "cls"), pairs)

    x, e, peak, total = local_stats(logits)
    mine = jnp.stack([peak, total])
    stats = [mine]
    for shift in range(1, n_cls):
        stats.append(lax.ppermute(mine, "cls", [(i, (i + shift) % n_cls) for i in range(n_cls)]))
    hot_cols, hot_rows, classes = index_forms(width, leaf_index, labels)

    planes = n_rows == 16 and n_cls == 2 and blocks == 4
    order = [(3, 3), (1, 1), (2, 2), (0, 0)] if planes else list(range(blocks))
    where = [(planes, d) for d in order]
    scale = None
    parts = []
    for block in where:
        if scale is None:
            part, scale = leaf_sums(block, e, hot_cols, classes, stats=stats)
        else:
            part = leaf_sums(block, e, hot_cols, classes, scale=scale, after=parts[-1])
        parts.append(part)

    if planes:
        got = [swap(part, far) for part, far in zip(parts[:3], order[:3])]
        sums = parts[3]
        for part in got:
            sums = lax.optimization_barrier(sums + part)
        for far in ((4, 8), (8, 4)):
            sums = sums + swap(sums, far)
        value = newton(sums)
        values = [swap(value, far) for far in order[:3]] + [value]
    else:
        values = [newton(s) for s in lax.psum(parts, "rows")]

    if planes:
        held = apply_blocks(where[3:], values[3:], x, hot_rows)
        held = apply_blocks(where[:1], values[:1], x, hot_rows, held)
        held = apply_blocks(where[1:3], values[1:3], x, hot_rows, held)
    else:
        held = apply_blocks(where, values, x, hot_rows)
    return held[0], held[1]


def solution(mesh):
    return jax.shard_map(
        functools.partial(per_device, mesh.shape["rows"], mesh.shape["cls"]),
        mesh=mesh,
        in_specs=(P("rows", "cls"), P("rows"), P("rows")),
        out_specs=(P(None, "cls"), P("rows", "cls")),
        check_vma=False,
    )
```

```python
import functools

import jax
import jax.numpy as jnp
from jax import lax
from jax.experimental import pallas as pl
from jax.experimental.pallas import tpu as pltpu
from jax.sharding import PartitionSpec as P

LEAVES = 128
LANE = 128
MIB = 2**20
F32 = jnp.float32
BF16 = jnp.bfloat16
IN_VMEM = pl.BlockSpec(memory_space=pltpu.VMEM)
IN_ANY = pl.BlockSpec(memory_space=pl.ANY)


def split(value):
    high = value.astype(BF16)
    return high, (value - high.astype(F32)).astype(BF16)


def params(limit):
    return pltpu.CompilerParams(vmem_limit_bytes=limit * MIB)


def stats_body(chunks, x_hbm, x_ref, e_ref, m_ref, s_ref, sems):
    step = x_hbm.shape[0] // chunks

    def fetch(i):
        at = pl.ds(i * step, step)
        return pltpu.make_async_copy(x_hbm.at[at], x_ref.at[at], sems.at[i])

    for i in range(chunks):
        fetch(i).start()
    diagonal = lax.broadcasted_iota(jnp.int32, (LANE, LANE), 0) == lax.broadcasted_iota(jnp.int32, (LANE, LANE), 1)
    for i in range(chunks):
        fetch(i).wait()
        for t in range(step // LANE):
            row = i * (step // LANE) + t
            at = pl.ds(row * LANE, LANE)
            x = x_ref[at]
            m = jnp.max(x, axis=1, keepdims=True)
            e = jnp.exp(x - m)
            s = jnp.sum(e, axis=1, keepdims=True)
            e_ref[at] = e
            m_ref[pl.ds(row, 1)] = jnp.sum(jnp.where(diagonal, m, 0.0), axis=0, keepdims=True)
            s_ref[pl.ds(row, 1)] = jnp.sum(jnp.where(diagonal, s, 0.0), axis=0, keepdims=True)


def local_stats(logits):
    rows, width = logits.shape
    chunks = 8
    full = pltpu.VMEM((rows, width), F32)
    small = jax.ShapeDtypeStruct((rows // LANE, LANE), F32)
    return pl.pallas_call(
        functools.partial(stats_body, chunks),
        out_shape=[full, full, small, small],
        in_specs=[IN_ANY],
        out_specs=[IN_VMEM] * 4,
        scratch_shapes=[pltpu.SemaphoreType.DMA((chunks,))],
        compiler_params=params(36),
        cost_estimate=pl.CostEstimate(flops=6 * rows * width, bytes_accessed=4 * rows * width, transcendentals=rows * width),
        name="local_stats",
    )(logits)


def index_body(width, leaf_ref, label_ref, cols_ref, rows_ref, class_ref):
    offset = lax.axis_index("cls") * width
    sub = lax.broadcasted_iota(jnp.int32, (LANE, LANE), 0)
    lane = lax.broadcasted_iota(jnp.int32, (LANE, LANE), 1)
    for t in range(leaf_ref.shape[0]):
        at = pl.ds(t * LANE, LANE)
        leaf = jnp.broadcast_to(leaf_ref[pl.ds(t, 1)], (LANE, LANE))
        label = jnp.broadcast_to(label_ref[pl.ds(t, 1)] - offset, (LANE, LANE))
        cols_ref[:, at] = jnp.where(sub == leaf, 1.0, 0.0).astype(BF16)
        rows_ref[at] = jnp.where(lane == leaf.T, 1.0, 0.0).astype(BF16)
        class_ref[at] = label.T


def index_forms(width, leaf_index, labels):
    rows = leaf_index.shape[0]
    shape = (rows // LANE, LANE)
    return pl.pallas_call(
        functools.partial(index_body, width),
        out_shape=[
            pltpu.VMEM((LEAVES, rows), BF16),
            pltpu.VMEM((rows, LEAVES), BF16),
            pltpu.VMEM((rows, LANE), jnp.int32),
        ],
        in_specs=[IN_VMEM, IN_VMEM],
        out_specs=[IN_VMEM] * 3,
        compiler_params=params(4),
        name="index_forms",
    )(leaf_index.reshape(shape), labels.reshape(shape))


def block_start(planes, block):
    if planes:
        far = jnp.where(lax.axis_index("cls") == 0, *block)
        return pl.multiple_of(((lax.axis_index("rows") & 3) ^ far) * LANE, LANE)
    return block * LANE


def sums_body(first, parties, place, e_ref, hot_ref, class_ref, *refs):
    if first:
        peaks, totals = refs[:parties], refs[parties : 2 * parties]
        out_ref, scale_ref, acc_ref = refs[2 * parties :]
        peak = functools.reduce(jnp.maximum, [p[...] for p in peaks])
        grown = [jnp.exp(p[...] - peak) for p in peaks]
        total = functools.reduce(jnp.add, [g * t[...] for g, t in zip(grown, totals)])
        factor = grown[0] / total
    else:
        scale_ref, _, out_ref, acc_ref = refs
    start = block_start(*place)
    columns = pl.ds(start, LANE)
    step = 512
    own = lax.broadcasted_iota(jnp.int32, (step, LANE), 1) + start
    for i in range(e_ref.shape[0] // step):
        at = pl.ds(i * step, step)
        if first:
            for t in range(step // LANE):
                row = i * (step // LANE) + t
                scale_ref[pl.ds(row * LANE, LANE)] = jnp.broadcast_to(factor[row : row + 1], (LANE, LANE)).T
        prob = e_ref[at, columns] * scale_ref[at]
        grad = jnp.where(class_ref[at] == own, prob - 1.0, prob)
        hess = prob * (1.0 - prob)
        right = jnp.concatenate(split(grad) + split(hess), axis=1)
        part = jnp.dot(hot_ref[:, at], right, preferred_element_type=F32)
        if i == 0:
            acc_ref[...] = part
        else:
            acc_ref[...] += part
    out_ref[:LEAVES] = acc_ref[:, :LANE] + acc_ref[:, LANE : 2 * LANE]
    out_ref[LEAVES:] = acc_ref[:, 2 * LANE : 3 * LANE] + acc_ref[:, 3 * LANE :]


def leaf_sums(place, e, hot, classes, scale=None, stats=None, after=None):
    rows = e.shape[0]
    first = scale is None
    out = [jax.ShapeDtypeStruct((2 * LEAVES, LANE), F32)]
    if first:
        out.append(pltpu.VMEM((rows, LANE), F32))
        more = [s[0] for s in stats] + [s[1] for s in stats]
    else:
        more = [scale, after]
    got = pl.pallas_call(
        functools.partial(sums_body, first, len(more) // 2, place),
        out_shape=out,
        in_specs=[IN_VMEM] * (3 + len(more)),
        out_specs=[IN_VMEM] * len(out),
        scratch_shapes=[pltpu.VMEM((LEAVES, 4 * LANE), F32)],
        compiler_params=params(6),
        cost_estimate=pl.CostEstimate(flops=1, bytes_accessed=1, transcendentals=0),
        name="leaf_sums",
    )(e, hot, classes, *more)
    return got if first else got[0]


def apply_body(first, sizes, places, x_ref, hot_ref, *refs):
    count, chunks = len(places), len(sizes)
    starts = [sum(sizes[:i]) for i in range(chunks)]
    values, refs = refs[:count], refs[count:]
    if not first:
        refs = refs[2:]
    value_hbm, updated_hbm, tile_ref, sems, value_sems = refs
    columns = [pl.ds(block_start(*place), LANE) for place in places]

    def send(i, b):
        at = pl.ds(starts[i], sizes[i])
        return pltpu.make_async_copy(tile_ref.at[b, at], updated_hbm.at[at, columns[b]], sems.at[i, b])

    def send_value(b):
        return pltpu.make_async_copy(values[b], value_hbm.at[:, columns[b]], value_sems.at[b])

    for b in range(count):
        send_value(b).start()
    right = [jnp.concatenate(split(value[...]), axis=0) for value in values]
    for i in range(chunks):
        at = pl.ds(starts[i], sizes[i])
        hot = hot_ref[at]
        left = jnp.concatenate([hot, hot], axis=1)
        for b in range(count):
            tile_ref[b, at] = x_ref[at, columns[b]] + jnp.dot(left, right[b], preferred_element_type=F32)
            send(i, b).start()
    for i in range(chunks):
        for b in range(count):
            send(i, b).wait()
    for b in range(count):
        send_value(b).wait()


def apply_blocks(places, values, x, hot, held=None):
    rows, width = x.shape
    count = len(places)
    step = 4 * LANE
    sizes = [LANE, step - LANE] + [step] * (rows // step - 2) + [step - LANE, LANE]
    first = held is None
    more = [] if first else list(held)
    return pl.pallas_call(
        functools.partial(apply_body, first, sizes, places),
        out_shape=[jax.ShapeDtypeStruct((LEAVES, width), F32), jax.ShapeDtypeStruct((rows, width), F32)],
        in_specs=[IN_VMEM] * (2 + count) + [IN_ANY] * len(more),
        out_specs=[IN_ANY] * 2,
        scratch_shapes=[
            pltpu.VMEM((count, rows, LANE), F32),
            pltpu.SemaphoreType.DMA((len(sizes), count)),
            pltpu.SemaphoreType.DMA((count,)),
        ],
        input_output_aliases={} if first else {2 + count: 0, 3 + count: 1},
        compiler_params=params(4 + 3 * count),
        cost_estimate=pl.CostEstimate(
            flops=4 * count * rows * LEAVES * LANE, bytes_accessed=4 * count * rows * LANE, transcendentals=0
        ),
        name="apply_blocks",
    )(x, hot, *values, *more)


def newton(sums):
    return -0.3 * sums[:LEAVES] / (sums[LEAVES:] + 1.0)


def per_device(n_rows, n_cls, logits, leaf_index, labels):
    width = logits.shape[1]
    blocks = width // LANE

    def swap(value, far):
        pairs = [(row * n_cls + core, (row ^ far[core]) * n_cls + core) for row in range(n_rows) for core in range(n_cls)]
        return lax.ppermute(value, ("rows", "cls"), pairs)

    x, e, peak, total = local_stats(logits)
    mine = jnp.stack([peak, total])
    stats = [mine]
    for shift in range(1, n_cls):
        stats.append(lax.ppermute(mine, "cls", [(i, (i + shift) % n_cls) for i in range(n_cls)]))
    hot_cols, hot_rows, classes = index_forms(width, leaf_index, labels)

    planes = n_rows == 16 and n_cls == 2 and blocks == 4
    order = [(3, 3), (1, 1), (2, 2), (0, 0)] if planes else list(range(blocks))
    where = [(planes, d) for d in order]
    scale = None
    parts = []
    for block in where:
        if scale is None:
            part, scale = leaf_sums(block, e, hot_cols, classes, stats=stats)
        else:
            part = leaf_sums(block, e, hot_cols, classes, scale=scale, after=parts[-1])
        parts.append(part)

    if planes:
        got = [swap(part, far) for part, far in zip(parts[:3], order[:3])]
        sums = parts[3]
        for part in got:
            sums = lax.optimization_barrier(sums + part)
        for far in ((4, 8), (8, 4)):
            sums = sums + swap(sums, far)
        value = newton(sums)
        values = [swap(value, far) for far in order[:3]] + [value]
    else:
        values = [newton(s) for s in lax.psum(parts, "rows")]

    if planes:
        held = apply_blocks(where[3:], values[3:], x, hot_rows)
        held = apply_blocks(where[:1], values[:1], x, hot_rows, held)
        held = apply_blocks(where[1:3], values[1:3], x, hot_rows, held)
    else:
        held = apply_blocks(where, values, x, hot_rows)
    return held[0], held[1]


def solution(mesh):
    return jax.shard_map(
        functools.partial(per_device, mesh.shape["rows"], mesh.shape["cls"]),
        mesh=mesh,
        in_specs=(P("rows", "cls"), P("rows"), P("rows")),
        out_specs=(P(None, "cls"), P("rows", "cls")),
        check_vma=False,
    )
```

```python
import functools

import jax
import jax.numpy as jnp
from jax import lax
from jax.experimental import pallas as pl
from jax.experimental.pallas import tpu as pltpu
from jax.sharding import PartitionSpec as P

LEAVES = 128
LANE = 128
MIB = 2**20
F32 = jnp.float32
BF16 = jnp.bfloat16
IN_VMEM = pl.BlockSpec(memory_space=pltpu.VMEM)
IN_ANY = pl.BlockSpec(memory_space=pl.ANY)


def split(value):
    high = value.astype(BF16)
    return high, (value - high.astype(F32)).astype(BF16)


def params(limit):
    return pltpu.CompilerParams(vmem_limit_bytes=limit * MIB)


def stats_body(chunks, x_hbm, x_ref, e_ref, m_ref, s_ref, sems):
    step = x_hbm.shape[0] // chunks

    def fetch(i):
        at = pl.ds(i * step, step)
        return pltpu.make_async_copy(x_hbm.at[at], x_ref.at[at], sems.at[i])

    for i in range(chunks):
        fetch(i).start()
    diagonal = lax.broadcasted_iota(jnp.int32, (LANE, LANE), 0) == lax.broadcasted_iota(jnp.int32, (LANE, LANE), 1)
    for i in range(chunks):
        fetch(i).wait()
        for t in range(step // LANE):
            row = i * (step // LANE) + t
            at = pl.ds(row * LANE, LANE)
            x = x_ref[at]
            m = jnp.max(x, axis=1, keepdims=True)
            e = jnp.exp(x - m)
            s = jnp.sum(e, axis=1, keepdims=True)
            e_ref[at] = e
            m_ref[pl.ds(row, 1)] = jnp.sum(jnp.where(diagonal, m, 0.0), axis=0, keepdims=True)
            s_ref[pl.ds(row, 1)] = jnp.sum(jnp.where(diagonal, s, 0.0), axis=0, keepdims=True)


def local_stats(logits):
    rows, width = logits.shape
    chunks = 8
    full = pltpu.VMEM((rows, width), F32)
    small = jax.ShapeDtypeStruct((rows // LANE, LANE), F32)
    return pl.pallas_call(
        functools.partial(stats_body, chunks),
        out_shape=[full, full, small, small],
        in_specs=[IN_ANY],
        out_specs=[IN_VMEM] * 4,
        scratch_shapes=[pltpu.SemaphoreType.DMA((chunks,))],
        compiler_params=params(36),
        cost_estimate=pl.CostEstimate(flops=6 * rows * width, bytes_accessed=4 * rows * width, transcendentals=rows * width),
        name="local_stats",
    )(logits)


def index_body(width, leaf_ref, label_ref, cols_ref, rows_ref, class_ref):
    offset = lax.axis_index("cls") * width
    sub = lax.broadcasted_iota(jnp.int32, (LANE, LANE), 0)
    lane = lax.broadcasted_iota(jnp.int32, (LANE, LANE), 1)
    for t in range(leaf_ref.shape[0]):
        at = pl.ds(t * LANE, LANE)
        leaf = jnp.broadcast_to(leaf_ref[pl.ds(t, 1)], (LANE, LANE))
        label = jnp.broadcast_to(label_ref[pl.ds(t, 1)] - offset, (LANE, LANE))
        cols_ref[:, at] = jnp.where(sub == leaf, 1.0, 0.0).astype(BF16)
        rows_ref[at] = jnp.where(lane == leaf.T, 1.0, 0.0).astype(BF16)
        class_ref[at] = label.T


def index_forms(width, leaf_index, labels):
    rows = leaf_index.shape[0]
    shape = (rows // LANE, LANE)
    return pl.pallas_call(
        functools.partial(index_body, width),
        out_shape=[
            pltpu.VMEM((LEAVES, rows), BF16),
            pltpu.VMEM((rows, LEAVES), BF16),
            pltpu.VMEM((rows, LANE), jnp.int32),
        ],
        in_specs=[IN_VMEM, IN_VMEM],
        out_specs=[IN_VMEM] * 3,
        compiler_params=params(4),
        name="index_forms",
    )(leaf_index.reshape(shape), labels.reshape(shape))


def block_start(planes, block):
    if planes:
        far = jnp.where(lax.axis_index("cls") == 0, *block)
        return pl.multiple_of(((lax.axis_index("rows") & 3) ^ far) * LANE, LANE)
    return block * LANE


def sums_body(first, parties, place, e_ref, hot_ref, class_ref, *refs):
    if first:
        peaks, totals = refs[:parties], refs[parties : 2 * parties]
        out_ref, scale_ref, acc_ref = refs[2 * parties :]
        peak = functools.reduce(jnp.maximum, [p[...] for p in peaks])
        grown = [jnp.exp(p[...] - peak) for p in peaks]
        total = functools.reduce(jnp.add, [g * t[...] for g, t in zip(grown, totals)])
        factor = grown[0] / total
    else:
        scale_ref, _, out_ref, acc_ref = refs
    start = block_start(*place)
    columns = pl.ds(start, LANE)
    step = 512
    own = lax.broadcasted_iota(jnp.int32, (step, LANE), 1) + start
    for i in range(e_ref.shape[0] // step):
        at = pl.ds(i * step, step)
        if first:
            for t in range(step // LANE):
                row = i * (step // LANE) + t
                scale_ref[pl.ds(row * LANE, LANE)] = jnp.broadcast_to(factor[row : row + 1], (LANE, LANE)).T
        prob = e_ref[at, columns] * scale_ref[at]
        grad = jnp.where(class_ref[at] == own, prob - 1.0, prob)
        hess = prob * (1.0 - prob)
        right = jnp.concatenate(split(grad) + split(hess), axis=1)
        part = jnp.dot(hot_ref[:, at], right, preferred_element_type=F32)
        if i == 0:
            acc_ref[...] = part
        else:
            acc_ref[...] += part
    out_ref[:LEAVES] = acc_ref[:, :LANE] + acc_ref[:, LANE : 2 * LANE]
    out_ref[LEAVES:] = acc_ref[:, 2 * LANE : 3 * LANE] + acc_ref[:, 3 * LANE :]


def leaf_sums(place, e, hot, classes, scale=None, stats=None, after=None):
    rows = e.shape[0]
    first = scale is None
    out = [jax.ShapeDtypeStruct((2 * LEAVES, LANE), F32)]
    if first:
        out.append(pltpu.VMEM((rows, LANE), F32))
        more = [s[0] for s in stats] + [s[1] for s in stats]
    else:
        more = [scale, after]
    got = pl.pallas_call(
        functools.partial(sums_body, first, len(more) // 2, place),
        out_shape=out,
        in_specs=[IN_VMEM] * (3 + len(more)),
        out_specs=[IN_VMEM] * len(out),
        scratch_shapes=[pltpu.VMEM((LEAVES, 4 * LANE), F32)],
        compiler_params=params(6),
        cost_estimate=pl.CostEstimate(flops=1, bytes_accessed=1, transcendentals=0),
        name="leaf_sums",
    )(e, hot, classes, *more)
    return got if first else got[0]


def apply_body(first, sizes, places, x_ref, hot_ref, *refs):
    count, chunks = len(places), len(sizes)
    starts = [sum(sizes[:i]) for i in range(chunks)]
    values, refs = refs[:count], refs[count:]
    if not first:
        refs = refs[2:]
    value_hbm, updated_hbm, tile_ref, sems, value_sems = refs
    columns = [pl.ds(block_start(*place), LANE) for place in places]

    def send(i, b):
        at = pl.ds(starts[i], sizes[i])
        return pltpu.make_async_copy(tile_ref.at[b, at], updated_hbm.at[at, columns[b]], sems.at[i, b])

    def send_value(b):
        return pltpu.make_async_copy(values[b], value_hbm.at[:, columns[b]], value_sems.at[b])

    for b in range(count):
        send_value(b).start()
    right = [jnp.concatenate(split(value[...]), axis=0) for value in values]
    for i in range(chunks):
        at = pl.ds(starts[i], sizes[i])
        hot = hot_ref[at]
        left = jnp.concatenate([hot, hot], axis=1)
        for b in range(count):
            tile_ref[b, at] = x_ref[at, columns[b]] + jnp.dot(left, right[b], preferred_element_type=F32)
            send(i, b).start()
    for i in range(chunks):
        for b in range(count):
            send(i, b).wait()
    for b in range(count):
        send_value(b).wait()


def apply_blocks(places, values, x, hot, held=None):
    rows, width = x.shape
    count = len(places)
    step = 4 * LANE
    sizes = [LANE, step - LANE] + [step] * (rows // step - 2) + [step - LANE, LANE]
    first = held is None
    more = [] if first else list(held)
    return pl.pallas_call(
        functools.partial(apply_body, first, sizes, places),
        out_shape=[jax.ShapeDtypeStruct((LEAVES, width), F32), jax.ShapeDtypeStruct((rows, width), F32)],
        in_specs=[IN_VMEM] * (2 + count) + [IN_ANY] * len(more),
        out_specs=[IN_ANY] * 2,
        scratch_shapes=[
            pltpu.VMEM((count, rows, LANE), F32),
            pltpu.SemaphoreType.DMA((len(sizes), count)),
            pltpu.SemaphoreType.DMA((count,)),
        ],
        input_output_aliases={} if first else {2 + count: 0, 3 + count: 1},
        compiler_params=params(4 + 3 * count),
        cost_estimate=pl.CostEstimate(
            flops=4 * count * rows * LEAVES * LANE, bytes_accessed=4 * count * rows * LANE, transcendentals=0
        ),
        name="apply_blocks",
    )(x, hot, *values, *more)


def newton(sums):
    return -0.3 * sums[:LEAVES] / (sums[LEAVES:] + 1.0)


def per_device(n_rows, n_cls, logits, leaf_index, labels):
    width = logits.shape[1]
    blocks = width // LANE

    def swap(value, far):
        pairs = [(row * n_cls + core, (row ^ far[core]) * n_cls + core) for row in range(n_rows) for core in range(n_cls)]
        return lax.ppermute(value, ("rows", "cls"), pairs)

    x, e, peak, total = local_stats(logits)
    mine = jnp.stack([peak, total])
    stats = [mine]
    for shift in range(1, n_cls):
        stats.append(lax.ppermute(mine, "cls", [(i, (i + shift) % n_cls) for i in range(n_cls)]))
    hot_cols, hot_rows, classes = index_forms(width, leaf_index, labels)

    planes = n_rows == 16 and n_cls == 2 and blocks == 4
    order = [(3, 3), (1, 1), (2, 2), (0, 0)] if planes else list(range(blocks))
    where = [(planes, d) for d in order]
    scale = None
    parts = []
    for block in where:
        if scale is None:
            part, scale = leaf_sums(block, e, hot_cols, classes, stats=stats)
        else:
            part = leaf_sums(block, e, hot_cols, classes, scale=scale, after=parts[-1])
        parts.append(part)

    if planes:
        got = [swap(part, far) for part, far in zip(parts[:3], order[:3])]
        sums = parts[3]
        for part in got:
            sums = lax.optimization_barrier(sums + part)
        for far in ((4, 8), (8, 4)):
            sums = sums + swap(sums, far)
        value = newton(sums)
        gather = [(1, 1), (2, 2), (3, 3)]
        values = [value] + [swap(value, far) for far in gather]
        where = [(planes, far) for far in [(0, 0)] + gather]
    else:
        values = [newton(s) for s in lax.psum(parts, "rows")]

    if planes:
        held = apply_blocks(where[:2], values[:2], x, hot_rows)
        held = apply_blocks(where[2:], values[2:], x, hot_rows, held)
    else:
        held = apply_blocks(where, values, x, hot_rows)
    return held[0], held[1]


def solution(mesh):
    return jax.shard_map(
        functools.partial(per_device, mesh.shape["rows"], mesh.shape["cls"]),
        mesh=mesh,
        in_specs=(P("rows", "cls"), P("rows"), P("rows")),
        out_specs=(P(None, "cls"), P("rows", "cls")),
        check_vma=False,
    )
```
